512 devices in a mesh: rows: 16 (over z, core), cols: 32 (over y, x).
Axes of the slice: x: 4, y: 8, z: 8, core: 2. Of those that a mesh axis runs over, the one named last changes fastest.
Arguments:
- genotypes: bfloat16 [491520, 2048], P(('rows', 'cols')), may hold values from 0 to 2
- probes: bfloat16 [491520, 128], P(('rows', 'cols')), may hold values from -6 to 6
- missing_codes: int32 [491520], P(('rows', 'cols')), may hold values from 0 to 31
Outputs:
- basis: bfloat16 [491520, 128], P(('rows', 'cols'))
- scores: bfloat16 [2048, 128], replicated
The draws below stay inside these ranges and needn't reach their ends.
Inputs may be any that keep to these rules, and one draw needn't show every extreme that they name: `missing_codes`: A code c below 16 marks SNPs c * 128 to (c + 1) * 128 - 1 as missing for that individual; larger codes mark none.
All inputs are finite; a program needn't handle non-finite values.
Results may differ from the reference program's by a relative error of at most 0.017.
Values sent between devices are 32-bit elements; how exact they have to be, the bound alone decides.
No kernel may reach another device: no remote copies, remote signals or barrier semaphores. Data moves between devices by JAX's collectives and lax.ppermute only.
A program may use at most 64 MiB of HBM per device.

```python
import math
import jax
import jax.numpy as jnp
from jax import lax

M = 2048
B = 128
BLOCK_SNPS = 128
NBLK = 16
NTOT = 491520
N_ROWS = 16


def draw_genotypes(key, part):
    key_freq, key_noise = jax.random.split(jax.random.fold_in(key, 17))
    lowest = 0.002
    freq = jnp.exp(jax.random.uniform(key_freq, (M,), jnp.float32, jnp.log(lowest), jnp.log(0.5)))
    ramp = 0.5 + jnp.arange(NTOT, dtype=jnp.float32) / NTOT
    effective = jnp.minimum(freq[None, :] * ramp[:, None], 0.75)
    spread = jnp.sqrt(2.0 * effective * (1.0 - effective))
    noise = jnp.clip(jax.random.normal(key_noise, (NTOT, M), jnp.float32), -3.0, 3.0)
    return jnp.clip(2.0 * effective + spread * noise, 0.0, 2.0).astype(jnp.bfloat16)


def with_ends(values, own_key, least, top_value):
    longest = values.shape.index(max(values.shape))
    spots = []
    for shift in (0, 1):
        where = [jax.random.randint(jax.random.fold_in(own_key, axis), (), 0, length) for axis, length in enumerate(values.shape)]
        where[longest] = (where[longest] + shift) % values.shape[longest]
        spots.append(tuple(where))
    return values.at[spots[0]].set(least).at[spots[1]].set(top_value)


def shard_levels(key, shape, cuts, smallest, top_value):
    loudness = 1.0
    for position, blocks in cuts:
        draws = jax.random.uniform(jax.random.fold_in(jax.random.fold_in(key, 6), position), (blocks,), jnp.float32, smallest / len(cuts), top_value / len(cuts))
        loudness = loudness * jnp.repeat(jnp.exp(draws), shape[position] // blocks).reshape((-1,) + (1,) * (len(shape) - 1 - position))
    return loudness


def gaussian(key, extent, scale, bound, cuts=(), kind=jnp.bfloat16):
    entries = scale * jax.random.normal(key, extent, jnp.float32)
    if cuts:
        entries = entries * shard_levels(key, extent, cuts, -0.22, 0.18)
    return jnp.clip(entries, -bound, bound).astype(kind)


def setup_inputs(seed: int = 0) -> dict:
    key_of = jax.random.split(jax.random.key(seed), 4)
    genotypes = draw_genotypes(jax.random.fold_in(key_of[3], 71), 0)
    probes = gaussian(key_of[1], (NTOT, B), 1.0, 6.0, ((0, 512),))
    missing_codes = with_ends(jax.random.randint(key_of[2], (NTOT,), 0, 2 * NBLK), jax.random.fold_in(key_of[2], 1), 0, (2 * NBLK) - 1).astype(jnp.int32)
    return dict(genotypes=genotypes, probes=probes, missing_codes=missing_codes)


def standardize(geno, codes, mean, inv_sd):
    snp_block = (jnp.arange(M) // BLOCK_SNPS).astype(jnp.int32)
    observed = (snp_block[None, :] != codes[:, None]).astype(jnp.float32)
    return ((geno.astype(jnp.float32) - mean[None, :]) * inv_sd[None, :] * observed).astype(jnp.bfloat16)

def reference(genotypes, probes, missing_codes):
    pieces = N_ROWS
    rows_block = NTOT // pieces
    geno_all = genotypes.reshape(pieces, rows_block, M)
    probe_all = probes.reshape(pieces, rows_block, B)
    code_all = missing_codes.reshape(pieces, rows_block)
    snp_block = (jnp.arange(M) // BLOCK_SNPS).astype(jnp.int32)

    def moment_step(accum, item):
        geno, codes = item
        observed = (snp_block[None, :] != codes[:, None]).astype(jnp.float32)
        dosage = geno.astype(jnp.float32) * observed
        part = jnp.stack([lax.optimization_barrier(jnp.sum(observed, 0)), lax.optimization_barrier(jnp.sum(dosage, 0)), lax.optimization_barrier(jnp.sum(dosage * dosage, 0))])
        return (accum + part, None)
    moments, _ = lax.scan(moment_step, jnp.zeros((3, M), jnp.float32), (geno_all, code_all))
    counted = jnp.maximum(moments[0], 1.0)
    mean = moments[1] / counted
    inv_sd = 1.0 / jnp.sqrt(moments[2] / counted - mean * mean + 1e-05)

    def project_step(accum, item):
        geno, codes, probe = item
        standard = standardize(geno, codes, mean, inv_sd)
        part = jnp.einsum('rs,rb->sb', standard.astype(jnp.float32), probe.astype(jnp.float32), precision=lax.Precision.HIGHEST)
        return (accum + part, None)
    projection, _ = lax.scan(project_step, jnp.zeros((M, B), jnp.float32), (geno_all, code_all, probe_all))
    projection = (projection / math.sqrt(NTOT)).astype(jnp.bfloat16)

    def image_step(accum, item):
        geno, codes = item
        standard = standardize(geno, codes, mean, inv_sd)
        image = (jnp.dot(standard.astype(jnp.float32), projection.astype(jnp.float32), preferred_element_type=jnp.float32) / math.sqrt(M)).astype(jnp.bfloat16)
        wide = image.astype(jnp.float32)
        gram = jnp.einsum('rb,rc->bc', wide, wide, precision=lax.Precision.HIGHEST)
        cross = jnp.einsum('rs,rb->sb', standard.astype(jnp.float32), wide, precision=lax.Precision.HIGHEST)
        return ((accum[0] + gram, accum[1] + cross), image)
    start = (jnp.zeros((B, B), jnp.float32), jnp.zeros((M, B), jnp.float32))
    (gram, cross), images = lax.scan(image_step, start, (geno_all, code_all))
    images = images.reshape(NTOT, B)
    lower = jnp.linalg.cholesky(gram)
    basis = jax.scipy.linalg.solve_triangular(lower, images.astype(jnp.float32).T, lower=True).T * math.sqrt(NTOT)
    scores = jax.scipy.linalg.solve_triangular(lower, cross.T, lower=True).T * math.sqrt(M / NTOT)
    return (basis.astype(jnp.bfloat16), scores.astype(jnp.bfloat16))
```

```python
import math

import jax
import jax.numpy as jnp
from jax import lax
from jax.sharding import Mesh
from jax.sharding import PartitionSpec as P

BLOCK_SNPS = 128
ALL = ("z", "c", "y", "x")
SWAP = ((0, 1), (1, 0))


def exchanged(blocks, axis):
    return lax.all_to_all(blocks, axis, 0, 0, tiled=True)


def summed_parts(array, axis):
    size = lax.axis_size(axis)
    blocks = array.reshape(size, array.shape[0] // size, array.shape[1])
    return jnp.sum(exchanged(blocks, axis), 0)


def copies(array, axis):
    return exchanged(jnp.broadcast_to(array[None], (lax.axis_size(axis), *array.shape)), axis)


def swapped(array):
    return lax.ppermute(array, "c", SWAP)


def per_device(genotypes, probes, missing_codes):
    rows, snps = genotypes.shape
    probe_count = probes.shape[1]
    total_rows = rows * math.prod(lax.axis_size(a) for a in ALL)
    core = lax.axis_index("c")
    blocks = snps // BLOCK_SNPS
    half = snps // 2
    block_half = blocks // 2
    wide_x, wide_y = lax.axis_size("x"), lax.axis_size("y")

    snp_block = jnp.arange(snps) // BLOCK_SNPS
    seen = snp_block[None, :] != missing_codes[:, None]
    observed = seen.astype(jnp.float32)
    kept = jnp.where(seen, genotypes, jnp.zeros_like(genotypes))
    dosage = kept.astype(jnp.float32)
    raw = jnp.einsum("rs,rb->sb", kept, probes, preferred_element_type=jnp.float32)
    total = jnp.sum(dosage, 0).reshape(blocks, BLOCK_SNPS)
    square = jnp.sum(dosage * dosage, 0).reshape(blocks, BLOCK_SNPS)
    by_block = jnp.arange(blocks)[None, :] != missing_codes[:, None]
    seen_probes = jnp.einsum(
        "rk,rb->kb", by_block.astype(jnp.bfloat16), probes, preferred_element_type=jnp.float32
    )
    count = jnp.broadcast_to(
        jnp.sum(by_block.astype(jnp.float32), 0)[:, None], (blocks, BLOCK_SNPS)
    )

    def part(which):
        def take(a):
            n = a.shape[0] // 2
            return lax.dynamic_slice_in_dim(a, which * n, n)

        return jnp.concatenate([take(a) for a in (raw, total, square, seen_probes, count)])

    mine = part(core) + swapped(part(1 - core))
    mine = summed_parts(mine, "x")
    mine = summed_parts(mine, "y")
    mine = jnp.sum(copies(mine, "z"), 0)
    mine = copies(mine, "y").reshape(-1, probe_count)
    mine = copies(mine, "x").reshape(-1, probe_count)
    other = swapped(mine)
    first = jnp.where(core == 0, mine, other)
    second = jnp.where(core == 0, other, mine)

    def joined(start, length):
        return jnp.concatenate([first[start : start + length], second[start : start + length]])

    raw = joined(0, half)
    total, square, seen_probes, count = (
        joined(half + i * block_half, block_half) for i in range(4)
    )
    counted = jnp.maximum(count, 1.0)
    mean = total / counted
    inv_sd = 1.0 / jnp.sqrt(square / counted - mean * mean + 1e-05)
    centred = (
        raw.reshape(blocks, BLOCK_SNPS, probe_count) - mean[:, :, None] * seen_probes[:, None, :]
    )
    projection = (centred * inv_sd[:, :, None] / math.sqrt(total_rows)).astype(jnp.bfloat16)
    projection = projection.reshape(snps, probe_count)
    standard = (
        (genotypes.astype(jnp.float32) - mean.reshape(1, snps)) * inv_sd.reshape(1, snps) * observed
    ).astype(jnp.bfloat16)
    image = (
        jnp.dot(standard, projection, preferred_element_type=jnp.float32) / math.sqrt(snps)
    ).astype(jnp.bfloat16)
    gram = jnp.einsum("rb,rc->bc", image, image, preferred_element_type=jnp.float32)
    cross = jnp.einsum("rs,rb->sb", standard, image, preferred_element_type=jnp.float32)

    def halves(which):
        n = probe_count // 2
        return jnp.concatenate(
            [
                lax.dynamic_slice_in_dim(cross, which * half, half),
                lax.dynamic_slice_in_dim(gram, which * n, n),
            ]
        )

    mine = halves(core) + swapped(halves(1 - core))
    over_x = jnp.concatenate(
        [
            mine[:half].reshape(wide_x, half // wide_x, probe_count),
            jnp.broadcast_to(mine[None, half:], (wide_x, probe_count // 2, probe_count)),
        ],
        1,
    )
    mine = jnp.sum(exchanged(over_x, "x"), 0)
    shard = half // wide_x
    over_y = jnp.concatenate(
        [
            mine[:shard].reshape(wide_y, shard // wide_y, probe_count),
            mine[shard:].reshape(wide_y, probe_count // 2 // wide_y, probe_count),
        ],
        1,
    )
    mine = jnp.sum(exchanged(over_y, "y"), 0)
    mine = jnp.sum(copies(mine, "z"), 0)
    back = copies(mine, "y")
    shard_y = shard // wide_y
    gram_half = back[:, shard_y:].reshape(probe_count // 2, probe_count)
    cross_half = copies(back[:, :shard_y].reshape(shard, probe_count), "x").reshape(
        half, probe_count
    )
    gram_other = swapped(gram_half)
    gram = jnp.where(
        core == 0,
        jnp.concatenate([gram_half, gram_other]),
        jnp.concatenate([gram_other, gram_half]),
    )
    lower = jnp.linalg.cholesky(gram)
    inverse = jax.scipy.linalg.solve_triangular(
        lower, jnp.eye(probe_count, dtype=jnp.float32), lower=True
    )
    basis = jnp.dot(image.astype(jnp.float32), inverse.T, precision=lax.Precision.HIGHEST)
    cross_other = swapped(cross_half)
    cross = jnp.where(
        core == 0,
        jnp.concatenate([cross_half, cross_other]),
        jnp.concatenate([cross_other, cross_half]),
    )
    scores = jnp.dot(cross, inverse.T, precision=lax.Precision.HIGHEST)
    return (
        (basis * math.sqrt(total_rows)).astype(jnp.bfloat16),
        (scores * math.sqrt(snps / total_rows)).astype(jnp.bfloat16),
    )


def solution(mesh):
    finer = Mesh(mesh.devices.reshape(8, 2, 8, 4), ALL)
    spec = (P(ALL, None), P(ALL, None), P(ALL))
    return jax.shard_map(
        per_device, mesh=finer, in_specs=spec, out_specs=(P(ALL, None), P()), check_vma=False
    )
```

```python
import math

import jax
import jax.numpy as jnp
from jax import lax
from jax.experimental import pallas as pl
from jax.experimental.pallas import tpu as pltpu
from jax.sharding import Mesh
from jax.sharding import PartitionSpec as P

BLOCK_SNPS = 128
ALL = ("z", "c", "y", "x")
SWAP = ((0, 1), (1, 0))


def exchanged(blocks, axis):
    return lax.all_to_all(blocks, axis, 0, 0, tiled=True)


def summed_parts(array, axis):
    size = lax.axis_size(axis)
    blocks = array.reshape(size, array.shape[0] // size, array.shape[1])
    return jnp.sum(exchanged(blocks, axis), 0)


def copies(array, axis):
    return exchanged(jnp.broadcast_to(array[None], (lax.axis_size(axis), *array.shape)), axis)


def swapped(array):
    return lax.ppermute(array, "c", SWAP)

def inverse_factor(gram):
    n = gram.shape[0]
    step = 8
    left = gram
    inv = (
        lax.broadcasted_iota(jnp.int32, (n, n), 0) == lax.broadcasted_iota(jnp.int32, (n, n), 1)
    ).astype(jnp.float32)
    row_of = lax.broadcasted_iota(jnp.int32, (step, n), 0)
    done = []
    for base in range(0, n, step):
        upper = left[:step]
        under = inv[:step]
        a = [
            [
                jnp.broadcast_to(upper[i : i + 1, base + k : base + k + 1], (step, n))
                if k >= i
                else None
                for k in range(step)
            ]
            for i in range(step)
        ]
        x = [[None] * step for _ in range(step)]
        scale = []
        for t in range(step):
            r = lax.rsqrt(a[t][t])
            scale.append(r)
            u = [None] * step
            for k in range(t + 1, step):
                u[k] = a[t][k] * r
            for i in range(t + 1, step):
                for k in range(i, step):
                    a[i][k] = a[i][k] - u[i] * u[k]
            a[t] = u
        for i in range(step):
            x[i][i] = scale[i]
            for k in range(i):
                s = a[k][i] * x[k][k]
                for m in range(k + 1, i):
                    s = s + a[m][i] * x[m][k]
                x[i][k] = -s * scale[i]
        cols = []
        for k in range(step):
            col = jnp.zeros((step, n), jnp.float32)
            for i in range(k, step):
                col = jnp.where(row_of == i, x[i][k], col)
            cols.append(col)
        both = jnp.concatenate([upper, under], 1)
        out = sum(
            jnp.concatenate([cols[k], cols[k]], 1) * both[k : k + 1] for k in range(step)
        )
        done.append(out[:, n:])
        if base + step < n:
            u = out[:, :n]
            prod = lax.dot_general(
                u, out, (((0,), (0,)), ((), ())), precision=lax.Precision.HIGHEST, preferred_element_type=jnp.float32
            )
            left = left[step:] - prod[base + step :, :n]
            inv = inv[step:] - prod[base + step :, n:]
    return jnp.concatenate(done, 0)


def inverse_kernel(near_ref, far_ref, core_ref, inverse_ref):
    first = core_ref[0] == 0
    near, far = near_ref[...], far_ref[...]
    gram = jnp.concatenate([jnp.where(first, near, far), jnp.where(first, far, near)], 0)
    gram = (gram + gram.T) * 0.5
    inverse_ref[...] = inverse_factor(gram)


def inverse_of_factor(near, far, core):
    n = near.shape[1]
    return pl.pallas_call(
        inverse_kernel,
        out_shape=jax.ShapeDtypeStruct((n, n), jnp.float32),
        in_specs=[
            pl.BlockSpec(memory_space=pltpu.VMEM),
            pl.BlockSpec(memory_space=pltpu.VMEM),
            pl.BlockSpec(memory_space=pltpu.SMEM),
        ],
        out_specs=pl.BlockSpec(memory_space=pltpu.VMEM),
        compiler_params=pltpu.CompilerParams(vmem_limit_bytes=32 * 2**20),
        cost_estimate=pl.CostEstimate(
            flops=9_000_000_000, bytes_accessed=1_000_000, transcendentals=128
        ),
    )(near, far, core.reshape(1))


def per_device(genotypes, probes, missing_codes):
    rows, snps = genotypes.shape
    probe_count = probes.shape[1]
    total_rows = rows * math.prod(lax.axis_size(a) for a in ALL)
    core = lax.axis_index("c")
    blocks = snps // BLOCK_SNPS
    half = snps // 2
    block_half = blocks // 2
    wide_x, wide_y = lax.axis_size("x"), lax.axis_size("y")

    snp_block = jnp.arange(snps) // BLOCK_SNPS
    seen = snp_block[None, :] != missing_codes[:, None]
    observed = seen.astype(jnp.float32)
    kept = jnp.where(seen, genotypes, jnp.zeros_like(genotypes))
    dosage = kept.astype(jnp.float32)
    raw = jnp.einsum("rs,rb->sb", kept, probes, preferred_element_type=jnp.float32)
    total = jnp.sum(dosage, 0).reshape(blocks, BLOCK_SNPS)
    square = jnp.sum(dosage * dosage, 0).reshape(blocks, BLOCK_SNPS)
    by_block = jnp.arange(blocks)[None, :] != missing_codes[:, None]
    seen_probes = jnp.einsum(
        "rk,rb->kb", by_block.astype(jnp.bfloat16), probes, preferred_element_type=jnp.float32
    )
    count = jnp.broadcast_to(
        jnp.sum(by_block.astype(jnp.float32), 0)[:, None], (blocks, BLOCK_SNPS)
    )

    def part(which):
        def take(a):
            n = a.shape[0] // 2
            return lax.dynamic_slice_in_dim(a, which * n, n)

        return jnp.concatenate([take(a) for a in (raw, total, square, seen_probes, count)])

    mine = part(core) + swapped(part(1 - core))
    mine = summed_parts(mine, "x")
    mine = summed_parts(mine, "y")
    mine = jnp.sum(copies(mine, "z"), 0)
    mine = copies(mine, "y").reshape(-1, probe_count)
    mine = copies(mine, "x").reshape(-1, probe_count)
    other = swapped(mine)
    first = jnp.where(core == 0, mine, other)
    second = jnp.where(core == 0, other, mine)

    def joined(start, length):
        return jnp.concatenate([first[start : start + length], second[start : start + length]])

    raw = joined(0, half)
    total, square, seen_probes, count = (
        joined(half + i * block_half, block_half) for i in range(4)
    )
    counted = jnp.maximum(count, 1.0)
    mean = total / counted
    inv_sd = 1.0 / jnp.sqrt(square / counted - mean * mean + 1e-05)
    centred = (
        raw.reshape(blocks, BLOCK_SNPS, probe_count) - mean[:, :, None] * seen_probes[:, None, :]
    )
    projection = (centred * inv_sd[:, :, None] / math.sqrt(total_rows)).astype(jnp.bfloat16)
    projection = projection.reshape(snps, probe_count)
    standard = (
        (genotypes.astype(jnp.float32) - mean.reshape(1, snps)) * inv_sd.reshape(1, snps) * observed
    ).astype(jnp.bfloat16)
    image = (
        jnp.dot(standard, projection, preferred_element_type=jnp.float32) / math.sqrt(snps)
    ).astype(jnp.bfloat16)
    gram = jnp.einsum("rb,rc->bc", image, image, preferred_element_type=jnp.float32)
    cross = jnp.einsum("rs,rb->sb", standard, image, preferred_element_type=jnp.float32)

    def halves(which):
        n = probe_count // 2
        return jnp.concatenate(
            [
                lax.dynamic_slice_in_dim(cross, which * half, half),
                lax.dynamic_slice_in_dim(gram, which * n, n),
            ]
        )

    mine = halves(core) + swapped(halves(1 - core))
    over_x = jnp.concatenate(
        [
            mine[:half].reshape(wide_x, half // wide_x, probe_count),
            jnp.broadcast_to(mine[None, half:], (wide_x, probe_count // 2, probe_count)),
        ],
        1,
    )
    mine = jnp.sum(exchanged(over_x, "x"), 0)
    shard = half // wide_x
    over_y = jnp.concatenate(
        [
            mine[:shard].reshape(wide_y, shard // wide_y, probe_count),
            mine[shard:].reshape(wide_y, probe_count // 2 // wide_y, probe_count),
        ],
        1,
    )
    mine = jnp.sum(exchanged(over_y, "y"), 0)
    mine = jnp.sum(copies(mine, "z"), 0)
    back = copies(mine, "y")
    shard_y = shard // wide_y
    gram_half = back[:, shard_y:].reshape(probe_count // 2, probe_count)
    cross_half = copies(back[:, :shard_y].reshape(shard, probe_count), "x").reshape(
        half, probe_count
    )
    gram_other = swapped(gram_half)
    inverse = inverse_of_factor(gram_half, gram_other, core)
    cross_half, inverse = lax.optimization_barrier((cross_half, inverse))
    cross_other = swapped(cross_half)
    cross = jnp.where(
        core == 0,
        jnp.concatenate([cross_half, cross_other]),
        jnp.concatenate([cross_other, cross_half]),
    )
    basis = jnp.dot(image.astype(jnp.float32), inverse.T, precision=lax.Precision.HIGHEST)
    scores = jnp.dot(cross, inverse.T, precision=lax.Precision.HIGHEST)
    return (
        (basis * math.sqrt(total_rows)).astype(jnp.bfloat16),
        (scores * math.sqrt(snps / total_rows)).astype(jnp.bfloat16),
    )


def solution(mesh):
    finer = Mesh(mesh.devices.reshape(8, 2, 8, 4), ALL)
    spec = (P(ALL, None), P(ALL, None), P(ALL))
    return jax.shard_map(
        per_device, mesh=finer, in_specs=spec, out_specs=(P(ALL, None), P()), check_vma=False
    )
```

```python
import math

import jax
import jax.numpy as jnp
from jax import lax
from jax.experimental import pallas as pl
from jax.experimental.pallas import tpu as pltpu
from jax.sharding import Mesh
from jax.sharding import PartitionSpec as P

BLOCK_SNPS = 128
ALL = ("z", "c", "y", "x")
SWAP = ((0, 1), (1, 0))


def exchanged(blocks, axis):
    return lax.all_to_all(blocks, axis, 0, 0, tiled=True)


def summed_parts(array, axis):
    size = lax.axis_size(axis)
    blocks = array.reshape(size, array.shape[0] // size, array.shape[1])
    return jnp.sum(exchanged(blocks, axis), 0)


def copies(array, axis):
    return exchanged(jnp.broadcast_to(array[None], (lax.axis_size(axis), *array.shape)), axis)


def swapped(array):
    return lax.ppermute(array, "c", SWAP)

def inverse_factor(gram):
    n = gram.shape[0]
    step = 8
    left = gram
    inv = (
        lax.broadcasted_iota(jnp.int32, (n, n), 0) == lax.broadcasted_iota(jnp.int32, (n, n), 1)
    ).astype(jnp.float32)
    row_of = lax.broadcasted_iota(jnp.int32, (step, n), 0)
    done = []
    for base in range(0, n, step):
        upper = left[:step]
        under = inv[:step]
        a = [
            [
                jnp.broadcast_to(upper[i : i + 1, base + k : base + k + 1], (step, n))
                if k >= i
                else None
                for k in range(step)
            ]
            for i in range(step)
        ]
        x = [[None] * step for _ in range(step)]
        scale = []
        for t in range(step):
            r = lax.rsqrt(a[t][t])
            scale.append(r)
            u = [None] * step
            for k in range(t + 1, step):
                u[k] = a[t][k] * r
            for i in range(t + 1, step):
                for k in range(i, step):
                    a[i][k] = a[i][k] - u[i] * u[k]
            a[t] = u
        for i in range(step):
            x[i][i] = scale[i]
            for k in range(i):
                s = a[k][i] * x[k][k]
                for m in range(k + 1, i):
                    s = s + a[m][i] * x[m][k]
                x[i][k] = -s * scale[i]
        cols = []
        for k in range(step):
            col = jnp.zeros((step, n), jnp.float32)
            for i in range(k, step):
                col = jnp.where(row_of == i, x[i][k], col)
            cols.append(col)
        both = jnp.concatenate([upper, under], 1)
        out = sum(
            jnp.concatenate([cols[k], cols[k]], 1) * both[k : k + 1] for k in range(step)
        )
        done.append(out[:, n:])
        if base + step < n:
            u = out[:, :n]
            prod = lax.dot_general(
                u, out, (((0,), (0,)), ((), ())), precision=lax.Precision.HIGHEST, preferred_element_type=jnp.float32
            )
            left = left[step:] - prod[base + step :, :n]
            inv = inv[step:] - prod[base + step :, n:]
    return jnp.concatenate(done, 0)


def inverse_kernel(near_ref, far_ref, core_ref, inverse_ref):
    first = core_ref[0] == 0
    near, far = near_ref[...], far_ref[...]
    gram = jnp.concatenate([jnp.where(first, near, far), jnp.where(first, far, near)], 0)
    gram = (gram + gram.T) * 0.5
    inverse_ref[...] = inverse_factor(gram)


def inverse_of_factor(near, far, core):
    n = near.shape[1]
    return pl.pallas_call(
        inverse_kernel,
        out_shape=jax.ShapeDtypeStruct((n, n), jnp.float32),
        in_specs=[
            pl.BlockSpec(memory_space=pltpu.VMEM),
            pl.BlockSpec(memory_space=pltpu.VMEM),
            pl.BlockSpec(memory_space=pltpu.SMEM),
        ],
        out_specs=pl.BlockSpec(memory_space=pltpu.VMEM),
        compiler_params=pltpu.CompilerParams(vmem_limit_bytes=32 * 2**20),
        cost_estimate=pl.CostEstimate(
            flops=9_000_000_000, bytes_accessed=1_000_000, transcendentals=128
        ),
    )(near, far, core.reshape(1))


VMEM = pltpu.CompilerParams(vmem_limit_bytes=48 * 2**20)
COLUMNS = 512
EXTRA = 32


def rows_sum(a, b):
    return lax.dot_general(a, b, (((0,), (0,)), ((), ())), preferred_element_type=jnp.float32)


def moments_kernel(half_ref, genotypes_ref, probes_ref, codes_ref, out_ref, codes_scratch):
    step = pl.program_id(0)
    per_step = COLUMNS // BLOCK_SNPS
    half_blocks = pl.num_programs(0) * per_step
    half = half_blocks * BLOCK_SNPS
    first_block = half_ref[0] * half_blocks
    rows = probes_ref.shape[0]

    @pl.when(step == 0)
    def _():
        codes_scratch[...] = jnp.broadcast_to(codes_ref[...], codes_scratch.shape)
        lane = lax.broadcasted_iota(jnp.int32, (rows, BLOCK_SNPS), 1)
        seen = (codes_scratch[...] != first_block + lane).astype(jnp.float32).astype(jnp.bfloat16)
        sums = rows_sum(seen, probes_ref[...])
        counts = rows_sum(seen, jnp.ones((rows, BLOCK_SNPS), jnp.bfloat16))
        out_ref[pl.ds(half + 2 * half_blocks, half_blocks)] = sums[:half_blocks]
        out_ref[pl.ds(half + 3 * half_blocks, half_blocks)] = counts[:half_blocks]

    for i in range(per_step):
        block = step * per_step + i
        seen = codes_scratch[...] != first_block + block
        dosage = jnp.where(
            seen, genotypes_ref[:, i * BLOCK_SNPS : (i + 1) * BLOCK_SNPS].astype(jnp.float32), 0.0
        )
        out_ref[pl.ds(pl.multiple_of(block * BLOCK_SNPS, BLOCK_SNPS), BLOCK_SNPS)] = rows_sum(
            dosage.astype(jnp.bfloat16), probes_ref[...]
        )
        out_ref[pl.ds(half + block, 1)] = jnp.sum(dosage, 0, keepdims=True)
        out_ref[pl.ds(half + half_blocks + block, 1)] = jnp.sum(dosage * dosage, 0, keepdims=True)


def moments(which, genotypes, probes, codes):
    rows, snps = genotypes.shape
    half = snps // 2
    steps = half // COLUMNS
    return pl.pallas_call(
        moments_kernel,
        grid_spec=pltpu.PrefetchScalarGridSpec(
            num_scalar_prefetch=1,
            grid=(steps,),
            in_specs=[
                pl.BlockSpec((rows, COLUMNS), lambda i, h: (0, h[0] * steps + i)),
                pl.BlockSpec(probes.shape, lambda i, h: (0, 0)),
                pl.BlockSpec(codes.shape, lambda i, h: (0, 0)),
            ],
            out_specs=pl.BlockSpec((half + EXTRA, BLOCK_SNPS), lambda i, h: (0, 0)),
            scratch_shapes=[pltpu.VMEM((rows, BLOCK_SNPS), jnp.int32)],
        ),
        out_shape=jax.ShapeDtypeStruct((half + EXTRA, BLOCK_SNPS), jnp.float32),
        compiler_params=VMEM,
        cost_estimate=pl.CostEstimate(
            flops=1_500_000_000, bytes_accessed=3_000_000, transcendentals=0
        ),
    )(which.reshape(1), genotypes, probes, codes)


def image_kernel(
    total_rows, core_ref, mine_ref, other_ref, genotypes_ref, codes_ref,
    standard_ref, image_ref, gram_ref, codes_scratch, projection, image_sum,
):
    step = pl.program_id(0)
    steps = pl.num_programs(0)
    per_step = COLUMNS // BLOCK_SNPS
    half_blocks = steps * per_step // 2
    half = half_blocks * BLOCK_SNPS
    snps = 2 * half

    @pl.when(step == 0)
    def _():
        codes_scratch[...] = jnp.broadcast_to(codes_ref[...], codes_scratch.shape)

    own = (core_ref[0] == 0) == (step < steps // 2)
    for i in range(per_step):
        block = step * per_step + i
        local = lax.rem(step, steps // 2) * per_step + i

        def row(start):
            at = pl.ds(start, 1)
            return jnp.where(own, mine_ref[at], other_ref[at])

        counted = jnp.maximum(row(half + 3 * half_blocks + local), 1.0)
        mean = row(half + local) / counted
        inv_sd = 1.0 / jnp.sqrt(
            row(half + half_blocks + local) / counted - mean * mean + 1e-05
        )
        square = (BLOCK_SNPS, BLOCK_SNPS)
        mean_down = jnp.broadcast_to(mean, square).T
        inv_sd_down = jnp.broadcast_to(inv_sd, square).T
        at = pl.ds(pl.multiple_of(local * BLOCK_SNPS, BLOCK_SNPS), BLOCK_SNPS)
        raw = jnp.where(own, mine_ref[at], other_ref[at])
        centred = raw - mean_down * row(half + 2 * half_blocks + local)
        here = slice(i * BLOCK_SNPS, (i + 1) * BLOCK_SNPS)
        projection[here] = (centred * inv_sd_down * (1.0 / math.sqrt(total_rows))).astype(
            jnp.bfloat16
        )
        scaled = (genotypes_ref[:, here].astype(jnp.float32) - mean) * inv_sd
        standard_ref[:, here] = jnp.where(codes_scratch[...] != block, scaled, 0.0).astype(
            jnp.bfloat16
        )
    part = jnp.dot(standard_ref[...], projection[...], preferred_element_type=jnp.float32)

    @pl.when(step == 0)
    def _():
        image_sum[...] = part

    @pl.when(step > 0)
    def _():
        image_sum[...] += part

    @pl.when(step == steps - 1)
    def _():
        image = (image_sum[...] * (1.0 / math.sqrt(snps))).astype(jnp.bfloat16)
        image_ref[...] = image
        gram_ref[...] = rows_sum(image, image)


def images(total_rows, core, mine, other, genotypes, codes):
    rows, snps = genotypes.shape
    probe_count = mine.shape[1]
    return pl.pallas_call(
        lambda *refs: image_kernel(total_rows, *refs),
        grid_spec=pltpu.PrefetchScalarGridSpec(
            num_scalar_prefetch=1,
            grid=(snps // COLUMNS,),
            in_specs=[
                pl.BlockSpec(mine.shape, lambda i, c: (0, 0)),
                pl.BlockSpec(other.shape, lambda i, c: (0, 0)),
                pl.BlockSpec((rows, COLUMNS), lambda i, c: (0, i)),
                pl.BlockSpec(codes.shape, lambda i, c: (0, 0)),
            ],
            out_specs=[
                pl.BlockSpec((rows, COLUMNS), lambda i, c: (0, i)),
                pl.BlockSpec((rows, probe_count), lambda i, c: (0, 0)),
                pl.BlockSpec((probe_count, probe_count), lambda i, c: (0, 0)),
            ],
            scratch_shapes=[
                pltpu.VMEM((rows, BLOCK_SNPS), jnp.int32),
                pltpu.VMEM((COLUMNS, probe_count), jnp.bfloat16),
                pltpu.VMEM((rows, probe_count), jnp.float32),
            ],
        ),
        out_shape=(
            jax.ShapeDtypeStruct((rows, snps), jnp.bfloat16),
            jax.ShapeDtypeStruct((rows, probe_count), jnp.bfloat16),
            jax.ShapeDtypeStruct((probe_count, probe_count), jnp.float32),
        ),
        compiler_params=VMEM,
        cost_estimate=pl.CostEstimate(
            flops=2_500_000_000, bytes_accessed=9_000_000, transcendentals=0
        ),
    )(core.reshape(1), mine, other, genotypes, codes)


def cross_kernel(which_ref, standard_ref, image_ref, gram_ref, out_ref):
    step = pl.program_id(0)
    out_ref[pl.ds(pl.multiple_of(step * COLUMNS, COLUMNS), COLUMNS)] = rows_sum(
        standard_ref[...], image_ref[...]
    )

    @pl.when(step == 0)
    def _():
        n = gram_ref.shape[0] // 2
        out_ref[pl.ds(pl.num_programs(0) * COLUMNS, n)] = gram_ref[
            pl.ds(pl.multiple_of(which_ref[0] * n, n), n)
        ]


def crossed(which, standard, image, gram):
    rows, snps = standard.shape
    half = snps // 2
    steps = half // COLUMNS
    n = image.shape[1]
    return pl.pallas_call(
        cross_kernel,
        grid_spec=pltpu.PrefetchScalarGridSpec(
            num_scalar_prefetch=1,
            grid=(steps,),
            in_specs=[
                pl.BlockSpec((rows, COLUMNS), lambda i, h: (0, h[0] * steps + i)),
                pl.BlockSpec(image.shape, lambda i, h: (0, 0)),
                pl.BlockSpec(gram.shape, lambda i, h: (0, 0)),
            ],
            out_specs=pl.BlockSpec((half + n // 2, n), lambda i, h: (0, 0)),
        ),
        out_shape=jax.ShapeDtypeStruct((half + n // 2, n), jnp.float32),
        compiler_params=VMEM,
        cost_estimate=pl.CostEstimate(
            flops=1_200_000_000, bytes_accessed=3_000_000, transcendentals=0
        ),
    )(which.reshape(1), standard, image, gram)


def per_device(genotypes, probes, missing_codes):
    rows, snps = genotypes.shape
    probe_count = probes.shape[1]
    total_rows = rows * math.prod(lax.axis_size(a) for a in ALL)
    core = lax.axis_index("c")
    half = snps // 2
    wide_x, wide_y = lax.axis_size("x"), lax.axis_size("y")
    codes = missing_codes.reshape(rows, 1)

    sent = moments(1 - core, genotypes, probes, codes)
    mine = moments(core, genotypes, probes, codes) + swapped(sent)
    mine = summed_parts(mine, "x")
    mine = summed_parts(mine, "y")
    mine = jnp.sum(copies(mine, "z"), 0)
    mine = copies(mine, "y").reshape(-1, probe_count)
    mine = copies(mine, "x").reshape(-1, probe_count)
    standard, image, gram = images(
        total_rows, core, mine, swapped(mine), genotypes, codes
    )
    sent = crossed(1 - core, standard, image, gram)
    mine = crossed(core, standard, image, gram) + swapped(sent)
    over_x = jnp.concatenate(
        [
            mine[:half].reshape(wide_x, half // wide_x, probe_count),
            jnp.broadcast_to(mine[None, half:], (wide_x, probe_count // 2, probe_count)),
        ],
        1,
    )
    mine = jnp.sum(exchanged(over_x, "x"), 0)
    shard = half // wide_x
    over_y = jnp.concatenate(
        [
            mine[:shard].reshape(wide_y, shard // wide_y, probe_count),
            mine[shard:].reshape(wide_y, probe_count // 2 // wide_y, probe_count),
        ],
        1,
    )
    mine = jnp.sum(exchanged(over_y, "y"), 0)
    mine = jnp.sum(copies(mine, "z"), 0)
    back = copies(mine, "y")
    shard_y = shard // wide_y
    gram_half = back[:, shard_y:].reshape(probe_count // 2, probe_count)
    cross_half = copies(back[:, :shard_y].reshape(shard, probe_count), "x").reshape(
        half, probe_count
    )
    gram_other = swapped(gram_half)
    inverse = inverse_of_factor(gram_half, gram_other, core)
    cross_half, inverse = lax.optimization_barrier((cross_half, inverse))
    cross_other = swapped(cross_half)
    cross = jnp.where(
        core == 0,
        jnp.concatenate([cross_half, cross_other]),
        jnp.concatenate([cross_other, cross_half]),
    )
    basis = jnp.dot(image.astype(jnp.float32), inverse.T, precision=lax.Precision.HIGHEST)
    scores = jnp.dot(cross, inverse.T, precision=lax.Precision.HIGHEST)
    return (
        (basis * math.sqrt(total_rows)).astype(jnp.bfloat16),
        (scores * math.sqrt(snps / total_rows)).astype(jnp.bfloat16),
    )


def solution(mesh):
    finer = Mesh(mesh.devices.reshape(8, 2, 8, 4), ALL)
    spec = (P(ALL, None), P(ALL, None), P(ALL))
    return jax.shard_map(
        per_device, mesh=finer, in_specs=spec, out_specs=(P(ALL, None), P()), check_vma=False
    )
```

```python
import math

import jax
import jax.numpy as jnp
from jax import lax
from jax.experimental import pallas as pl
from jax.experimental.pallas import tpu as pltpu
from jax.sharding import Mesh
from jax.sharding import PartitionSpec as P

BLOCK_SNPS = 128
ALL = ("z", "c", "y", "x")
SWAP = ((0, 1), (1, 0))


def exchanged(blocks, axis):
    return lax.all_to_all(blocks, axis, 0, 0, tiled=True)


def summed_parts(array, axis):
    size = lax.axis_size(axis)
    blocks = array.reshape(size, array.shape[0] // size, array.shape[1])
    return jnp.sum(exchanged(blocks, axis), 0)


def copies(array, axis):
    return exchanged(jnp.broadcast_to(array[None], (lax.axis_size(axis), *array.shape)), axis)


def swapped(array):
    return lax.ppermute(array, "c", SWAP)

def panel(upper, under, base, extra):
    step, n = upper.shape
    row_of = lax.broadcasted_iota(jnp.int32, (step, n), 0)
    a = [
        [
            jnp.broadcast_to(upper[i : i + 1, base + k : base + k + 1], (step, n))
            if k >= i
            else None
            for k in range(step)
        ]
        for i in range(step)
    ]
    x = [[None] * step for _ in range(step)]
    scale = []
    for t in range(step):
        r = lax.rsqrt(a[t][t])
        scale.append(r)
        u = [None] * step
        for k in range(t + 1, step):
            u[k] = a[t][k] * r
        for i in range(t + 1, step):
            for k in range(i, step):
                a[i][k] = a[i][k] - u[i] * u[k]
        a[t] = u
    for i in range(step):
        x[i][i] = scale[i]
        for k in range(i):
            s = a[k][i] * x[k][k]
            for m in range(k + 1, i):
                s = s + a[m][i] * x[m][k]
            x[i][k] = -s * scale[i]
    both = jnp.concatenate([upper, under], 1)
    out = None
    for k in range(step):
        col = jnp.zeros((step, n), jnp.float32)
        for i in range(k, step):
            col = jnp.where(row_of == i, x[i][k], col)
        term = jnp.concatenate([col, col], 1) * both[k : k + 1]
        out = term if out is None else out + term
    columns = None
    if extra is not None:
        raw = [jnp.broadcast_to(extra[:, base + k : base + k + 1], (step, n)) for k in range(step)]
        columns = []
        for t in range(step):
            s = raw[0] * x[t][0]
            for k in range(1, t + 1):
                s = s + raw[k] * x[t][k]
            columns.append(s)
    return out, columns


def inverse_factor(gram):
    n = gram.shape[0]
    step = 8
    left = gram
    inv = (
        lax.broadcasted_iota(jnp.int32, (n, n), 0) == lax.broadcasted_iota(jnp.int32, (n, n), 1)
    ).astype(jnp.float32)
    done = []
    for base in range(0, n, 2 * step):
        first, columns = panel(left[:step], inv[:step], base, left[step : 2 * step])
        both = jnp.concatenate([left[step : 2 * step], inv[step : 2 * step]], 1)
        for t in range(step):
            both = both - jnp.concatenate([columns[t], columns[t]], 1) * first[t : t + 1]
        second, _ = panel(both[:, :n], both[:, n:], base + step, None)
        out = jnp.concatenate([first, second], 0)
        done.append(out[:, n:])
        if base + 2 * step < n:
            prod = lax.dot_general(
                out[:, :n],
                out,
                (((0,), (0,)), ((), ())),
                precision=lax.Precision.HIGHEST,
                preferred_element_type=jnp.float32,
            )
            left = left[2 * step :] - prod[base + 2 * step :, :n]
            inv = inv[2 * step :] - prod[base + 2 * step :, n:]
    return jnp.concatenate(done, 0)


def inverse_kernel(near_ref, far_ref, core_ref, inverse_ref):
    first = core_ref[0] == 0
    near, far = near_ref[...], far_ref[...]
    gram = jnp.concatenate([jnp.where(first, near, far), jnp.where(first, far, near)], 0)
    gram = (gram + gram.T) * 0.5
    inverse_ref[...] = inverse_factor(gram)


def inverse_of_factor(near, far, core):
    n = near.shape[1]
    return pl.pallas_call(
        inverse_kernel,
        out_shape=jax.ShapeDtypeStruct((n, n), jnp.float32),
        in_specs=[
            pl.BlockSpec(memory_space=pltpu.VMEM),
            pl.BlockSpec(memory_space=pltpu.VMEM),
            pl.BlockSpec(memory_space=pltpu.SMEM),
        ],
        out_specs=pl.BlockSpec(memory_space=pltpu.VMEM),
        compiler_params=pltpu.CompilerParams(vmem_limit_bytes=32 * 2**20),
        cost_estimate=pl.CostEstimate(
            flops=9_000_000_000, bytes_accessed=1_000_000, transcendentals=128
        ),
    )(near, far, core.reshape(1))


VMEM = pltpu.CompilerParams(vmem_limit_bytes=60 * 2**20)
COLUMNS = 512
EXTRA = 32


def rows_sum(a, b):
    return lax.dot_general(a, b, (((0,), (0,)), ((), ())), preferred_element_type=jnp.float32)


def moments_kernel(half_ref, genotypes_ref, probes_ref, codes_ref, out_ref, codes_scratch):
    step = pl.program_id(0)
    per_step = COLUMNS // BLOCK_SNPS
    half_blocks = pl.num_programs(0) * per_step
    half = half_blocks * BLOCK_SNPS
    first_block = half_ref[0] * half_blocks
    rows = probes_ref.shape[0]

    @pl.when(step == 0)
    def _():
        codes_scratch[...] = jnp.broadcast_to(codes_ref[...], codes_scratch.shape)
        lane = lax.broadcasted_iota(jnp.int32, (rows, BLOCK_SNPS), 1)
        seen = (codes_scratch[...] != first_block + lane).astype(jnp.float32).astype(jnp.bfloat16)
        sums = rows_sum(seen, probes_ref[...])
        counts = rows_sum(seen, jnp.ones((rows, BLOCK_SNPS), jnp.bfloat16))
        out_ref[pl.ds(half + 2 * half_blocks, half_blocks)] = sums[:half_blocks]
        out_ref[pl.ds(half + 3 * half_blocks, half_blocks)] = counts[:half_blocks]

    for i in range(per_step):
        block = step * per_step + i
        seen = codes_scratch[...] != first_block + block
        dosage = jnp.where(
            seen, genotypes_ref[:, i * BLOCK_SNPS : (i + 1) * BLOCK_SNPS].astype(jnp.float32), 0.0
        )
        out_ref[pl.ds(pl.multiple_of(block * BLOCK_SNPS, BLOCK_SNPS), BLOCK_SNPS)] = rows_sum(
            dosage.astype(jnp.bfloat16), probes_ref[...]
        )
        out_ref[pl.ds(half + block, 1)] = jnp.sum(dosage, 0, keepdims=True)
        out_ref[pl.ds(half + half_blocks + block, 1)] = jnp.sum(dosage * dosage, 0, keepdims=True)


def moments(which, genotypes, probes, codes):
    rows, snps = genotypes.shape
    half = snps // 2
    steps = half // COLUMNS
    return pl.pallas_call(
        moments_kernel,
        grid_spec=pltpu.PrefetchScalarGridSpec(
            num_scalar_prefetch=1,
            grid=(steps,),
            in_specs=[
                pl.BlockSpec((rows, COLUMNS), lambda i, h: (0, h[0] * steps + i)),
                pl.BlockSpec(probes.shape, lambda i, h: (0, 0)),
                pl.BlockSpec(codes.shape, lambda i, h: (0, 0)),
            ],
            out_specs=pl.BlockSpec((half + EXTRA, BLOCK_SNPS), lambda i, h: (0, 0)),
            scratch_shapes=[pltpu.VMEM((rows, BLOCK_SNPS), jnp.int32)],
        ),
        out_shape=jax.ShapeDtypeStruct((half + EXTRA, BLOCK_SNPS), jnp.float32),
        compiler_params=VMEM,
        cost_estimate=pl.CostEstimate(
            flops=1_500_000_000, bytes_accessed=3_000_000, transcendentals=0
        ),
    )(which.reshape(1), genotypes, probes, codes)


def per_device(genotypes, probes, missing_codes):
    rows, snps = genotypes.shape
    probe_count = probes.shape[1]
    total_rows = rows * math.prod(lax.axis_size(a) for a in ALL)
    core = lax.axis_index("c")
    half = snps // 2
    wide_x, wide_y = lax.axis_size("x"), lax.axis_size("y")
    codes = missing_codes.reshape(rows, 1)

    sent = moments(1 - core, genotypes, probes, codes)
    mine = moments(core, genotypes, probes, codes) + swapped(sent)
    mine = summed_parts(mine, "x")
    mine = summed_parts(mine, "y")
    mine = jnp.sum(copies(mine, "z"), 0)
    mine = copies(mine, "y").reshape(-1, probe_count)
    mine = copies(mine, "x").reshape(-1, probe_count)
    other = swapped(mine)
    first = jnp.where(core == 0, mine, other)
    second = jnp.where(core == 0, other, mine)
    blocks = snps // BLOCK_SNPS
    block_half = blocks // 2

    def joined(start, length):
        return jnp.concatenate([first[start : start + length], second[start : start + length]])

    raw = joined(0, half)
    total, square, seen_probes, count = (
        joined(half + i * block_half, block_half) for i in range(4)
    )
    counted = jnp.maximum(count, 1.0)
    mean = total / counted
    inv_sd = 1.0 / jnp.sqrt(square / counted - mean * mean + 1e-05)
    centred = (
        raw.reshape(blocks, BLOCK_SNPS, probe_count) - mean[:, :, None] * seen_probes[:, None, :]
    )
    projection = (centred * inv_sd[:, :, None] / math.sqrt(total_rows)).astype(jnp.bfloat16)
    projection = projection.reshape(snps, probe_count)
    snp_block = jnp.arange(snps) // BLOCK_SNPS
    observed = (snp_block[None, :] != missing_codes[:, None]).astype(jnp.float32)
    standard = (
        (genotypes.astype(jnp.float32) - mean.reshape(1, snps)) * inv_sd.reshape(1, snps) * observed
    ).astype(jnp.bfloat16)
    image = (
        jnp.dot(standard, projection, preferred_element_type=jnp.float32) / math.sqrt(snps)
    ).astype(jnp.bfloat16)
    gram = jnp.einsum("rb,rc->bc", image, image, preferred_element_type=jnp.float32)
    cross = jnp.einsum("rs,rb->sb", standard, image, preferred_element_type=jnp.float32)

    def halves(which):
        n = probe_count // 2
        return jnp.concatenate(
            [
                lax.dynamic_slice_in_dim(cross, which * half, half),
                lax.dynamic_slice_in_dim(gram, which * n, n),
            ]
        )

    mine = halves(core) + swapped(halves(1 - core))
    over_x = jnp.concatenate(
        [
            mine[:half].reshape(wide_x, half // wide_x, probe_count),
            jnp.broadcast_to(mine[None, half:], (wide_x, probe_count // 2, probe_count)),
        ],
        1,
    )
    mine = jnp.sum(exchanged(over_x, "x"), 0)
    shard = half // wide_x
    over_y = jnp.concatenate(
        [
            mine[:shard].reshape(wide_y, shard // wide_y, probe_count),
            mine[shard:].reshape(wide_y, probe_count // 2 // wide_y, probe_count),
        ],
        1,
    )
    mine = jnp.sum(exchanged(over_y, "y"), 0)
    mine = jnp.sum(copies(mine, "z"), 0)
    back = copies(mine, "y")
    shard_y = shard // wide_y
    gram_half = back[:, shard_y:].reshape(probe_count // 2, probe_count)
    cross_half = copies(back[:, :shard_y].reshape(shard, probe_count), "x").reshape(
        half, probe_count
    )
    gram_other = swapped(gram_half)
    inverse = inverse_of_factor(gram_half, gram_other, core)
    cross_half, inverse = lax.optimization_barrier((cross_half, inverse))
    cross_other = swapped(cross_half)
    cross = jnp.where(
        core == 0,
        jnp.concatenate([cross_half, cross_other]),
        jnp.concatenate([cross_other, cross_half]),
    )
    basis = jnp.dot(image.astype(jnp.float32), inverse.T, precision=lax.Precision.HIGHEST)
    scores = jnp.dot(cross, inverse.T, precision=lax.Precision.HIGHEST)
    return (
        (basis * math.sqrt(total_rows)).astype(jnp.bfloat16),
        (scores * math.sqrt(snps / total_rows)).astype(jnp.bfloat16),
    )


def solution(mesh):
    finer = Mesh(mesh.devices.reshape(8, 2, 8, 4), ALL)
    spec = (P(ALL, None), P(ALL, None), P(ALL))
    return jax.shard_map(
        per_device, mesh=finer, in_specs=spec, out_specs=(P(ALL, None), P()), check_vma=False
    )
```

```python
import math

import jax
import jax.numpy as jnp
from jax import lax
from jax.experimental import pallas as pl
from jax.experimental.pallas import tpu as pltpu
from jax.sharding import Mesh
from jax.sharding import PartitionSpec as P

BLOCK_SNPS = 128
ALL = ("z", "c", "y", "x")
SWAP = ((0, 1), (1, 0))


def exchanged(blocks, axis):
    return lax.all_to_all(blocks, axis, 0, 0, tiled=True)


def flat_sum(array, axis):
    blocks = array.reshape(lax.axis_size(axis), 1, -1)
    return jnp.sum(exchanged(blocks, axis), 0)


def flat_copies(flat, axis):
    return exchanged(jnp.broadcast_to(flat[None], (lax.axis_size(axis), *flat.shape)), axis)


def summed_everywhere(array):
    shard = flat_sum(array, ("y", "x"))
    shard = jnp.sum(flat_copies(shard, "z"), 0)
    return flat_copies(shard, ("y", "x")).reshape(array.shape)


def swapped(array):
    return lax.ppermute(array, "c", SWAP)

def panel(upper, under, base, extra):
    step, n = upper.shape
    row_of = lax.broadcasted_iota(jnp.int32, (step, n), 0)
    a = [
        [
            jnp.broadcast_to(upper[i : i + 1, base + k : base + k + 1], (step, n))
            if k >= i
            else None
            for k in range(step)
        ]
        for i in range(step)
    ]
    x = [[None] * step for _ in range(step)]
    scale = []
    for t in range(step):
        r = lax.rsqrt(a[t][t])
        scale.append(r)
        u = [None] * step
        for k in range(t + 1, step):
            u[k] = a[t][k] * r
        for i in range(t + 1, step):
            for k in range(i, step):
                a[i][k] = a[i][k] - u[i] * u[k]
        a[t] = u
    for i in range(step):
        x[i][i] = scale[i]
        for k in range(i):
            s = a[k][i] * x[k][k]
            for m in range(k + 1, i):
                s = s + a[m][i] * x[m][k]
            x[i][k] = -s * scale[i]
    both = jnp.concatenate([upper, under], 1)
    out = None
    for k in range(step):
        col = jnp.zeros((step, n), jnp.float32)
        for i in range(k, step):
            col = jnp.where(row_of == i, x[i][k], col)
        term = jnp.concatenate([col, col], 1) * both[k : k + 1]
        out = term if out is None else out + term
    columns = None
    if extra is not None:
        raw = [jnp.broadcast_to(extra[:, base + k : base + k + 1], (step, n)) for k in range(step)]
        columns = []
        for t in range(step):
            s = raw[0] * x[t][0]
            for k in range(1, t + 1):
                s = s + raw[k] * x[t][k]
            columns.append(s)
    return out, columns


def inverse_factor(gram):
    n = gram.shape[0]
    step = 8
    left = gram
    inv = (
        lax.broadcasted_iota(jnp.int32, (n, n), 0) == lax.broadcasted_iota(jnp.int32, (n, n), 1)
    ).astype(jnp.float32)
    done = []
    for base in range(0, n, 2 * step):
        first, columns = panel(left[:step], inv[:step], base, left[step : 2 * step])
        both = jnp.concatenate([left[step : 2 * step], inv[step : 2 * step]], 1)
        for t in range(step):
            both = both - jnp.concatenate([columns[t], columns[t]], 1) * first[t : t + 1]
        second, _ = panel(both[:, :n], both[:, n:], base + step, None)
        out = jnp.concatenate([first, second], 0)
        done.append(out[:, n:])
        if base + 2 * step < n:
            prod = lax.dot_general(
                out[:, :n],
                out,
                (((0,), (0,)), ((), ())),
                precision=lax.Precision.HIGHEST,
                preferred_element_type=jnp.float32,
            )
            left = left[2 * step :] - prod[base + 2 * step :, :n]
            inv = inv[2 * step :] - prod[base + 2 * step :, n:]
    return jnp.concatenate(done, 0)


def inverse_kernel(scale, first_ref, second_ref, inverse_ref):
    gram = first_ref[...] + second_ref[...]
    inverse_ref[...] = inverse_factor((gram + gram.T) * (0.5 * scale))


def inverse_of_factor(scale, first, second):
    return pl.pallas_call(
        lambda *refs: inverse_kernel(scale, *refs),
        out_shape=jax.ShapeDtypeStruct(first.shape, jnp.float32),
        in_specs=[pl.BlockSpec(memory_space=pltpu.VMEM)] * 2,
        out_specs=pl.BlockSpec(memory_space=pltpu.VMEM),
        compiler_params=pltpu.CompilerParams(vmem_limit_bytes=32 * 2**20),
        cost_estimate=pl.CostEstimate(
            flops=6_000_000_000, bytes_accessed=1_000_000, transcendentals=128
        ),
    )(first, second)


def per_device(genotypes, probes, missing_codes):
    rows, snps = genotypes.shape
    probe_count = probes.shape[1]
    total_rows = rows * math.prod(lax.axis_size(a) for a in ALL)
    core = lax.axis_index("c")
    blocks = snps // BLOCK_SNPS
    half = snps // 2
    block_half = blocks // 2

    snp_block = jnp.arange(snps) // BLOCK_SNPS
    seen = snp_block[None, :] != missing_codes[:, None]
    observed = seen.astype(jnp.float32)
    kept = jnp.where(seen, genotypes, jnp.zeros_like(genotypes))
    dosage = kept.astype(jnp.float32)
    raw = jnp.einsum("rs,rb->sb", kept, probes, preferred_element_type=jnp.float32)
    total = jnp.sum(dosage, 0).reshape(blocks, BLOCK_SNPS)
    square = jnp.sum(dosage * dosage, 0).reshape(blocks, BLOCK_SNPS)
    by_block = jnp.arange(blocks)[None, :] != missing_codes[:, None]
    seen_probes = jnp.einsum(
        "rk,rb->kb", by_block.astype(jnp.bfloat16), probes, preferred_element_type=jnp.float32
    )
    count = jnp.broadcast_to(
        jnp.sum(by_block.astype(jnp.float32), 0)[:, None], (blocks, BLOCK_SNPS)
    )

    def part(which):
        def take(a):
            n = a.shape[0] // 2
            return lax.dynamic_slice_in_dim(a, which * n, n)

        return jnp.concatenate([take(a) for a in (raw, total, square, seen_probes, count)])

    mine = part(core) + swapped(part(1 - core))
    mine = summed_everywhere(mine)
    other = swapped(mine)
    first = jnp.where(core == 0, mine, other)
    second = jnp.where(core == 0, other, mine)

    def joined(start, length):
        return jnp.concatenate([first[start : start + length], second[start : start + length]])

    raw = joined(0, half)
    total, square, seen_probes, count = (
        joined(half + i * block_half, block_half) for i in range(4)
    )
    counted = jnp.maximum(count, 1.0)
    mean = total / counted
    inv_sd = 1.0 / jnp.sqrt(square / counted - mean * mean + 1e-05)
    centred = (
        raw.reshape(blocks, BLOCK_SNPS, probe_count) - mean[:, :, None] * seen_probes[:, None, :]
    )
    projection = (centred * inv_sd[:, :, None] / math.sqrt(total_rows)).astype(jnp.bfloat16)
    projection = projection.reshape(snps, probe_count)
    standard = (
        (genotypes.astype(jnp.float32) - mean.reshape(1, snps)) * inv_sd.reshape(1, snps) * observed
    ).astype(jnp.bfloat16)
    image = (
        jnp.dot(standard, projection, preferred_element_type=jnp.float32) / math.sqrt(snps)
    ).astype(jnp.bfloat16)
    cross = jnp.einsum("rs,rb->sb", standard, image, preferred_element_type=jnp.float32)

    def part_of(array, which):
        return lax.dynamic_slice_in_dim(array, which * half, half)

    mine = part_of(cross, core) + swapped(part_of(cross, 1 - core))
    mine = summed_everywhere(mine)
    other = swapped(mine)

    def gram_of(which, cross_half):
        return jnp.einsum(
            "sb,sc->bc",
            part_of(projection, which).astype(jnp.float32),
            cross_half,
            precision=lax.Precision.HIGHEST,
        )

    inverse = inverse_of_factor(
        1.0 / math.sqrt(snps), gram_of(core, mine), gram_of(1 - core, other)
    )
    basis = jnp.dot(image.astype(jnp.float32), inverse.T, precision=lax.Precision.HIGHEST)
    cross = jnp.where(
        core == 0, jnp.concatenate([mine, other]), jnp.concatenate([other, mine])
    )
    scores = jnp.dot(cross, inverse.T, precision=lax.Precision.HIGHEST)
    return (
        (basis * math.sqrt(total_rows)).astype(jnp.bfloat16),
        (scores * math.sqrt(snps / total_rows)).astype(jnp.bfloat16),
    )


def solution(mesh):
    finer = Mesh(mesh.devices.reshape(8, 2, 8, 4), ALL)
    spec = (P(ALL, None), P(ALL, None), P(ALL))
    return jax.shard_map(
        per_device, mesh=finer, in_specs=spec, out_specs=(P(ALL, None), P()), check_vma=False
    )
```

```python
import math

import jax
import jax.numpy as jnp
from jax import lax
from jax.experimental import pallas as pl
from jax.experimental.pallas import tpu as pltpu
from jax.sharding import Mesh
from jax.sharding import PartitionSpec as P

BLOCK_SNPS = 128
ALL = ("z", "c", "y", "x")
SWAP = ((0, 1), (1, 0))


def exchanged(blocks, axis):
    return lax.all_to_all(blocks, axis, 0, 0, tiled=True)


def blocks_of(array, size):
    rows = array.shape[0] // size
    if rows % 8:
        return array.reshape(size, 1, rows * array.shape[1])
    return array.reshape(size, rows, array.shape[1])


def copies(shard, axis):
    return exchanged(jnp.broadcast_to(shard[None], (lax.axis_size(axis), *shard.shape)), axis)


def summed_everywhere(array):
    near = ("y", "x")
    shard = jnp.sum(exchanged(blocks_of(array, lax.axis_size(near)), near), 0)
    shard = jnp.sum(copies(shard, "z"), 0)
    return copies(shard, near).reshape(array.shape)


def swapped(array):
    return lax.ppermute(array, "c", SWAP)

def panel(upper, under, base, extra):
    step, n = upper.shape
    row_of = lax.broadcasted_iota(jnp.int32, (step, n), 0)
    a = [
        [
            jnp.broadcast_to(upper[i : i + 1, base + k : base + k + 1], (step, n))
            if k >= i
            else None
            for k in range(step)
        ]
        for i in range(step)
    ]
    x = [[None] * step for _ in range(step)]
    scale = []
    for t in range(step):
        r = lax.rsqrt(a[t][t])
        scale.append(r)
        u = [None] * step
        for k in range(t + 1, step):
            u[k] = a[t][k] * r
        for i in range(t + 1, step):
            for k in range(i, step):
                a[i][k] = a[i][k] - u[i] * u[k]
        a[t] = u
    for i in range(step):
        x[i][i] = scale[i]
        for k in range(i):
            s = a[k][i] * x[k][k]
            for m in range(k + 1, i):
                s = s + a[m][i] * x[m][k]
            x[i][k] = -s * scale[i]
    both = jnp.concatenate([upper, under], 1)
    out = None
    for k in range(step):
        col = jnp.zeros((step, n), jnp.float32)
        for i in range(k, step):
            col = jnp.where(row_of == i, x[i][k], col)
        term = jnp.concatenate([col, col], 1) * both[k : k + 1]
        out = term if out is None else out + term
    columns = None
    if extra is not None:
        raw = [jnp.broadcast_to(extra[:, base + k : base + k + 1], (step, n)) for k in range(step)]
        columns = []
        for t in range(step):
            s = raw[0] * x[t][0]
            for k in range(1, t + 1):
                s = s + raw[k] * x[t][k]
            columns.append(s)
    return out, columns


def inverse_factor(gram):
    n = gram.shape[0]
    step = 8
    left = gram
    inv = (
        lax.broadcasted_iota(jnp.int32, (n, n), 0) == lax.broadcasted_iota(jnp.int32, (n, n), 1)
    ).astype(jnp.float32)
    done = []
    for base in range(0, n, 2 * step):
        first, columns = panel(left[:step], inv[:step], base, left[step : 2 * step])
        both = jnp.concatenate([left[step : 2 * step], inv[step : 2 * step]], 1)
        for t in range(step):
            both = both - jnp.concatenate([columns[t], columns[t]], 1) * first[t : t + 1]
        second, _ = panel(both[:, :n], both[:, n:], base + step, None)
        out = jnp.concatenate([first, second], 0)
        done.append(out[:, n:])
        if base + 2 * step < n:
            prod = lax.dot_general(
                out[:, :n],
                out,
                (((0,), (0,)), ((), ())),
                precision=lax.Precision.HIGHEST,
                preferred_element_type=jnp.float32,
            )
            left = left[2 * step :] - prod[base + 2 * step :, :n]
            inv = inv[2 * step :] - prod[base + 2 * step :, n:]
    return jnp.concatenate(done, 0)


def inverse_kernel(scale, first_ref, second_ref, inverse_ref):
    gram = first_ref[...] + second_ref[...]
    inverse_ref[...] = inverse_factor((gram + gram.T) * (0.5 * scale))


def inverse_of_factor(scale, first, second):
    return pl.pallas_call(
        lambda *refs: inverse_kernel(scale, *refs),
        out_shape=jax.ShapeDtypeStruct(first.shape, jnp.float32),
        in_specs=[pl.BlockSpec(memory_space=pltpu.VMEM)] * 2,
        out_specs=pl.BlockSpec(memory_space=pltpu.VMEM),
        compiler_params=pltpu.CompilerParams(vmem_limit_bytes=32 * 2**20),
        cost_estimate=pl.CostEstimate(
            flops=6_000_000_000, bytes_accessed=1_000_000, transcendentals=128
        ),
    )(first, second)


EXTRA = 32
CHUNK = 2 * BLOCK_SNPS
PADDED = 128
PIECES = 4


def padded_rows(array, rows):
    spare = rows - array.shape[0]
    if not spare:
        return array
    return jnp.concatenate([array, jnp.zeros((spare, array.shape[1]), array.dtype)], 0)


def moments_kernel(
    which_ref, genotypes_ref, probes_ref, codes_ref, out_ref, held, turned, code_down, semaphores
):
    rows, probe_count = probes_ref.shape
    half = held.shape[1]
    chunks = half // CHUNK
    half_blocks = half // BLOCK_SNPS
    which = which_ref[0]
    start = pl.multiple_of(which * half, half)
    copies_in = []
    pieces = semaphores.shape[0]
    length = rows // pieces
    for i in range(pieces):
        at = pl.ds(i * length, length)
        copy = pltpu.make_async_copy(
            genotypes_ref.at[at, pl.ds(start, half)], held.at[at], semaphores.at[i]
        )
        copy.start()
        copies_in.append(copy)

    long = turned.shape[1]
    probes = probes_ref[...]
    turned[pl.ds(0, probe_count)] = (
        padded_rows(probes.astype(jnp.float32), long).T.astype(jnp.bfloat16)
    )
    turned[pl.ds(probe_count, 16)] = jnp.ones((16, long), jnp.bfloat16)
    codes = codes_ref[...].astype(jnp.float32)
    first_block = (which * half_blocks).astype(jnp.float32)
    line = lax.broadcasted_iota(jnp.int32, (16, rows), 0).astype(jnp.float32)
    seen = (line + first_block != codes).astype(jnp.float32)
    sums = jnp.dot(seen.astype(jnp.bfloat16), probes, preferred_element_type=jnp.float32)
    counts = jnp.broadcast_to(jnp.sum(seen, 1, keepdims=True), (16, BLOCK_SNPS))
    out_ref[pl.ds(half + 2 * half_blocks, half_blocks)] = sums[:half_blocks]
    out_ref[pl.ds(half + 3 * half_blocks, half_blocks)] = counts[:half_blocks]
    if long > rows:
        codes = jnp.concatenate([codes, jnp.zeros((1, long - rows), jnp.float32)], 1)
    code_down[...] = jnp.broadcast_to(codes, (BLOCK_SNPS, long)).T

    for copy in copies_in:
        copy.wait()
    for i in range(chunks):
        kept = []
        for k in range(2):
            block = 2 * i + k
            at = pl.ds(block * BLOCK_SNPS, BLOCK_SNPS)
            dosage = jnp.where(
                code_down[pl.ds(0, rows)] != first_block + float(block),
                held[:, at].astype(jnp.float32),
                0.0,
            )
            out_ref[pl.ds(half + half_blocks + block, 1)] = jnp.sum(
                dosage * dosage, 0, keepdims=True
            )
            kept.append(dosage.astype(jnp.bfloat16))
        both = padded_rows(jnp.concatenate(kept, 1), long)
        product = jnp.dot(turned[...], both, preferred_element_type=jnp.float32)
        for k in range(2):
            block = 2 * i + k
            columns = slice(k * BLOCK_SNPS, (k + 1) * BLOCK_SNPS)
            out_ref[pl.ds(block * BLOCK_SNPS, BLOCK_SNPS)] = product[:probe_count, columns].T
            out_ref[pl.ds(half + block, 1)] = product[probe_count : probe_count + 1, columns]


def moments(which, genotypes, probes, codes, vmem):
    rows, snps = genotypes.shape
    half = snps // 2
    long = -(-rows // PADDED) * PADDED
    return pl.pallas_call(
        moments_kernel,
        in_specs=[
            pl.BlockSpec(memory_space=pltpu.SMEM),
            pl.BlockSpec(memory_space=pltpu.HBM),
            pl.BlockSpec(memory_space=pltpu.VMEM),
            pl.BlockSpec(memory_space=pltpu.VMEM),
        ],
        out_specs=pl.BlockSpec(memory_space=pltpu.VMEM),
        scratch_shapes=[
            pltpu.VMEM((rows, half), jnp.bfloat16),
            pltpu.VMEM((probes.shape[1] + 16, long), jnp.bfloat16),
            pltpu.VMEM((long, BLOCK_SNPS), jnp.float32),
            pltpu.SemaphoreType.DMA((PIECES,)),
        ],
        out_shape=jax.ShapeDtypeStruct((half + EXTRA, BLOCK_SNPS), jnp.float32),
        compiler_params=pltpu.CompilerParams(vmem_limit_bytes=vmem * 2**20),
        cost_estimate=pl.CostEstimate(
            flops=1_500_000_000, bytes_accessed=3_000_000, transcendentals=0
        ),
    )(which.reshape(1), genotypes, probes, codes)


def per_device(genotypes, probes, missing_codes):
    rows, snps = genotypes.shape
    probe_count = probes.shape[1]
    total_rows = rows * math.prod(lax.axis_size(a) for a in ALL)
    core = lax.axis_index("c")
    blocks = snps // BLOCK_SNPS
    half = snps // 2
    block_half = blocks // 2

    snp_block = jnp.arange(snps) // BLOCK_SNPS
    seen = snp_block[None, :] != missing_codes[:, None]
    observed = seen.astype(jnp.float32)
    codes = missing_codes.reshape(1, rows)
    sent = moments(1 - core, genotypes, probes, codes, 56)
    mine = moments(core, genotypes, probes, codes, 32) + swapped(sent)
    mine = summed_everywhere(mine)
    other = swapped(mine)
    first = jnp.where(core == 0, mine, other)
    second = jnp.where(core == 0, other, mine)

    def joined(start, length):
        return jnp.concatenate([first[start : start + length], second[start : start + length]])

    raw = joined(0, half)
    total, square, seen_probes, count = (
        joined(half + i * block_half, block_half) for i in range(4)
    )
    counted = jnp.maximum(count, 1.0)
    mean = total / counted
    inv_sd = 1.0 / jnp.sqrt(square / counted - mean * mean + 1e-05)
    centred = (
        raw.reshape(blocks, BLOCK_SNPS, probe_count) - mean[:, :, None] * seen_probes[:, None, :]
    )
    projection = (centred * inv_sd[:, :, None] / math.sqrt(total_rows)).astype(jnp.bfloat16)
    projection = projection.reshape(snps, probe_count)
    standard = (
        (genotypes.astype(jnp.float32) - mean.reshape(1, snps)) * inv_sd.reshape(1, snps) * observed
    ).astype(jnp.bfloat16)
    image = (
        jnp.dot(standard, projection, preferred_element_type=jnp.float32) / math.sqrt(snps)
    ).astype(jnp.bfloat16)
    cross = jnp.einsum("rs,rb->sb", standard, image, preferred_element_type=jnp.float32)

    def part_of(array, which):
        return lax.dynamic_slice_in_dim(array, which * half, half)

    mine = part_of(cross, core) + swapped(part_of(cross, 1 - core))
    mine = summed_everywhere(mine)
    other = swapped(mine)

    def gram_of(which, cross_half):
        return jnp.einsum(
            "sb,sc->bc",
            part_of(projection, which).astype(jnp.float32),
            cross_half,
            precision=lax.Precision.HIGHEST,
        )

    inverse = inverse_of_factor(
        1.0 / math.sqrt(snps), gram_of(core, mine), gram_of(1 - core, other)
    )
    basis = jnp.dot(image.astype(jnp.float32), inverse.T, precision=lax.Precision.HIGH)
    cross = jnp.where(
        core == 0, jnp.concatenate([mine, other]), jnp.concatenate([other, mine])
    )
    scores = jnp.dot(cross, inverse.T, precision=lax.Precision.HIGH)
    return (
        (basis * math.sqrt(total_rows)).astype(jnp.bfloat16),
        (scores * math.sqrt(snps / total_rows)).astype(jnp.bfloat16),
    )


def solution(mesh):
    finer = Mesh(mesh.devices.reshape(8, 2, 8, 4), ALL)
    spec = (P(ALL, None), P(ALL, None), P(ALL))
    return jax.shard_map(
        per_device, mesh=finer, in_specs=spec, out_specs=(P(ALL, None), P()), check_vma=False
    )
```
